32 devices in a mesh: row: 4 (over z), col: 8 (over y, x, core).
Axes of the slice: x: 2, y: 2, z: 4, core: 2. Of those that a mesh axis runs over, the one named last changes fastest.
Arguments:
- activations: bfloat16 [96, 48, 3072], P('row', None, 'col'), may hold values from -30 to 30
- cotangent: bfloat16 [96, 48, 3072], P('row', None, 'col'), may hold values from -6 to 6
- kernel: float32 [7, 7, 3072], P(None, None, 'col'), may hold values from -0.875 to 0.875
- ln_gain: float32 [3072], replicated, may hold values from 0.25 to 1.75
- ln_bias: float32 [3072], replicated, may hold values from -3 to 3
- w_expand: bfloat16 [3072, 12288], P('row', 'col'), may hold values from -0.5 to 0.5
- b_expand: float32 [12288], P('col'), may hold values from -3 to 3
- w_reduce: bfloat16 [12288, 3072], P('col', 'row'), may hold values from -0.078125 to 0.078125
- b_reduce: float32 [3072], P('col'), may hold values from -3 to 3
- layer_scale: float32 [3072], P('col'), may hold values from 0.3 to 1.5
Outputs:
- block_out: bfloat16 [96, 48, 3072], P('row', None, 'col')
- grad_input: bfloat16 [96, 48, 3072], P('row', None, 'col')
The draws below stay inside these ranges and needn't reach their ends.
All inputs are finite; a program needn't handle non-finite values.
Results may differ from the reference program's by a relative error of at most 0.015.
Values may be sent and summed in bfloat16 or wider, within the bound.
A program may use at most 128 MiB of HBM per device.

```python
import math
import jax
import jax.numpy as jnp
from jax import lax

B = 2
H = 48
W = 48
C = 3072
F = 12288
IMAGE_ROWS = 96
N_COL = 8


def draw_activations(key, part):
    first_key, second_key = jax.random.split(jax.random.fold_in(key, 17), 2)
    position = jnp.arange(C, dtype=jnp.float32) / C
    channel_ramp = 0.6 + 1.2 * position
    roughness = jnp.exp(jax.random.uniform(second_key, (C,), jnp.float32, -1.15, 1.15))
    values = jnp.clip(jax.random.normal(first_key, (B * H, W, C), jnp.float32), -5.0, 5.0)
    return (values * channel_ramp * roughness).astype(jnp.bfloat16)


def draw_w_expand(key, part):
    noise_key, order_key, common_key = jax.random.split(jax.random.fold_in(key, 29), 3)
    groups = N_COL
    order = jax.random.permutation(order_key, groups)
    chan_block = jnp.arange(C, dtype=jnp.int32) // (C // groups)
    unit_block = jnp.arange(F, dtype=jnp.int32) // (F // groups)
    paired = jnp.sum((unit_block[:, None] == jnp.arange(groups, dtype=jnp.int32)[None, :]).astype(jnp.int32) * order[None, :].astype(jnp.int32), 1)
    spiked = paired[None, :] == chan_block[:, None]
    factor = jnp.where(spiked, 3.0, 1.0).astype(jnp.float32)
    shared = jnp.clip(jax.random.normal(common_key, (F,), jnp.float32), -4.0, 4.0)
    noise = jnp.clip(jax.random.normal(noise_key, (C, F), jnp.float32), -6.0, 6.0)
    strength = 0.6
    values = (noise * factor + strength * shared[None, :]) / jnp.sqrt(jnp.float32(C))
    values = jnp.clip(values, -0.5, 0.5)
    return values.astype(jnp.bfloat16)


def strengthened(values, own_key, source, target, parts, factor):
    owner, partner = [(jnp.arange(values.shape[axis_at]) // (values.shape[axis_at] // parts)).reshape([-1 if axis == axis_at else 1 for axis in range(values.ndim)]) for axis_at in (source, target)]
    chosen = jax.random.permutation(own_key, parts)[partner]
    strong = (owner == chosen) | (owner == (partner + parts // 2) % parts)
    return jnp.where(strong, factor * values, values)


def block_levels(key, shape, cuts, least, top_value):
    factor_of = 1.0
    for dim, shards_of in cuts:
        steps = jax.random.uniform(jax.random.fold_in(jax.random.fold_in(key, 6), dim), (shards_of,), jnp.float32, least / len(cuts), top_value / len(cuts))
        factor_of = factor_of * jnp.repeat(jnp.exp(steps), shape[dim] // shards_of).reshape((-1,) + (1,) * (len(shape) - 1 - dim))
    return factor_of


def centred(stream_key, dims, deviation, reach, cuts=(), kind=jnp.bfloat16):
    array = deviation * jax.random.normal(stream_key, dims, jnp.float32)
    if cuts:
        array = array * block_levels(stream_key, dims, cuts, -0.22, 0.18)
    return jnp.clip(array, -reach, reach).astype(kind)


def bell_draw_with(rng, extent, spread, most, cuts, heavy, held_as=jnp.bfloat16):
    array = spread * jax.random.normal(rng, extent, jnp.float32)
    if cuts:
        array = array * block_levels(rng, extent, cuts, -0.22, 0.18)
    return jnp.clip(strengthened(array, jax.random.fold_in(rng, 3), *heavy), -most, most).astype(held_as)


def setup_inputs(seed: int = 0) -> dict:
    keys = jax.random.split(jax.random.key(seed), 11)
    return {
        "activations": draw_activations(jax.random.fold_in(keys[10], 71), 0),
        "cotangent": centred(keys[1], (IMAGE_ROWS, W, C), 1.0, 6.0, ((0, 4), (2, 8))),
        "kernel": centred(keys[2], (7, 7, C), 49 ** -0.5, 0.875, ((2, 8),), jnp.float32),
        "ln_gain": jnp.clip(1.0 + 0.15 * jax.random.normal(keys[3], (C,), jnp.float32), 0.25, 1.75),
        "ln_bias": centred(keys[4], (C,), 0.5, 3.0, (), jnp.float32),
        "w_expand": draw_w_expand(jax.random.fold_in(keys[10], 71), 0),
        "b_expand": centred(keys[6], (F,), 0.5, 3.0, ((0, 8),), jnp.float32),
        "w_reduce": bell_draw_with(keys[7], (F, C), F ** -0.5, 0.078125, ((0, 8), (1, 4)), (0, 1, 8, 2.0)),
        "b_reduce": centred(keys[8], (C,), 0.5, 3.0, ((0, 8),), jnp.float32),
        "layer_scale": jnp.clip(jnp.exp(math.log(1.5) - 1.60943787 * jax.random.uniform(keys[9], (C,), jnp.float32) ** block_levels(keys[9], (C,), ((0, 8),), -0.2, 0.2)), 0.3, 1.5),
    }


epsilon = 1e-06
root_half = 0.7071067811865476
density_scale = 0.3989422804014327

def spatial_mix(padded, weights, first_row, height):
    row_count = padded.shape[0] - 6
    col_count = padded.shape[1] - 6
    out_rows = first_row + jnp.arange(row_count, dtype=jnp.int32)
    running = jnp.zeros((row_count, col_count, padded.shape[2]), jnp.float32)
    for row_off in range(7):
        source = out_rows + (row_off - 3)
        inside = source // height == out_rows // height
        band = jnp.zeros_like(running)
        for col_off in range(7):
            band = band + weights[row_off, col_off] * padded[row_off:row_off + row_count, col_off:col_off + col_count]
        running = running + jnp.where(inside[:, None, None], band, jnp.zeros_like(band))
    return running

def gelu_slope(preact):
    cumulative = 0.5 * (1.0 + jax.scipy.special.erf(preact * root_half))
    return cumulative + preact * jnp.exp(-0.5 * preact * preact) * density_scale

def reference(activations, cotangent, kernel, ln_gain, ln_bias, w_expand, b_expand, w_reduce, b_reduce, layer_scale):
    row_total, grid_width, channels = activations.shape
    tokens = row_total * grid_width
    kernel_f = kernel.astype(jnp.float32)
    padded = jnp.pad(activations, ((3, 3), (3, 3), (0, 0))).astype(jnp.float32)
    mixed_bf = spatial_mix(padded, kernel_f, jnp.int32(0), H).astype(jnp.bfloat16)
    mixed_f = lax.optimization_barrier(mixed_bf).astype(jnp.float32).reshape(tokens, channels)
    row_mean = lax.optimization_barrier(jnp.sum(mixed_f, 1, keepdims=True)) / channels
    square = lax.optimization_barrier(jnp.sum(mixed_f * mixed_f, 1, keepdims=True)) / channels
    inv_std = lax.rsqrt(square - row_mean * row_mean + epsilon)
    normal = (mixed_f - row_mean) * inv_std
    normed = (normal * ln_gain + ln_bias).astype(jnp.bfloat16)
    preact = jnp.dot(normed, w_expand, preferred_element_type=jnp.float32) + b_expand
    hidden = jax.nn.gelu(preact, approximate=False).astype(jnp.bfloat16)
    branch_out = jnp.dot(hidden, w_reduce, preferred_element_type=jnp.float32) + b_reduce
    act_f = activations.astype(jnp.float32)
    block_out = (act_f + layer_scale * branch_out.reshape(row_total, grid_width, channels)).astype(jnp.bfloat16)
    cot_f = cotangent.astype(jnp.float32)
    grad_branch = (layer_scale * cot_f).reshape(tokens, channels).astype(jnp.bfloat16)
    grad_hidden = jnp.dot(grad_branch, w_reduce.T, preferred_element_type=jnp.float32)
    grad_preact = (grad_hidden * gelu_slope(preact)).astype(jnp.bfloat16)
    grad_normed = jnp.dot(grad_preact, w_expand.T, preferred_element_type=jnp.float32)
    grad_gain = grad_normed * ln_gain
    grad_total = lax.optimization_barrier(jnp.sum(grad_gain, 1, keepdims=True))
    grad_cross = lax.optimization_barrier(jnp.sum(grad_gain * normal, 1, keepdims=True))
    grad_mixed = inv_std * (grad_gain - grad_total / channels - normal * grad_cross / channels)
    grad_mixed = grad_mixed.astype(jnp.bfloat16).reshape(row_total, grid_width, channels)
    grad_padded = jnp.pad(grad_mixed, ((3, 3), (3, 3), (0, 0))).astype(jnp.float32)
    grad_spatial = spatial_mix(grad_padded, kernel_f[::-1, ::-1], jnp.int32(0), H).astype(jnp.bfloat16)
    grad_input = (cot_f + lax.optimization_barrier(grad_spatial).astype(jnp.float32)).astype(jnp.bfloat16)
    return (block_out, grad_input)
```

```python
import functools

import jax
import jax.numpy as jnp
from jax import lax
from jax.experimental import pallas as pl
from jax.experimental.pallas import tpu as pltpu
from jax.sharding import PartitionSpec as P

H = 48
LANES = 128
CHUNKS = 2

epsilon = 1e-06
root_half = 0.7071067811865476
density_scale = 0.3989422804014327


def conv_kernel(flip, add, x_ref, top_ref, bottom_ref, k_ref, *rest):
    if add:
        add_ref, o_ref, field = rest
    else:
        o_ref, field = rest
    rows, width, lanes = x_ref.shape
    field[...] = jnp.zeros_like(field)
    field[0:3, 8 : 8 + width, :] = top_ref[...].astype(jnp.float32)
    field[3 : 3 + rows, 8 : 8 + width, :] = x_ref[...].astype(jnp.float32)
    field[3 + rows : 6 + rows, 8 : 8 + width, :] = bottom_ref[...].astype(jnp.float32)

    @pl.loop(0, rows)
    def _(r):
        total = jnp.zeros((width, lanes), jnp.float32)
        for a in range(7):
            for b in range(7):
                weight = k_ref[6 - a, 6 - b] if flip else k_ref[a, b]
                total += weight[None, :] * field[r + a, 5 + b : 5 + b + width, :]
        mixed = total.astype(jnp.bfloat16)
        if add:
            mixed = (add_ref[r].astype(jnp.float32) + mixed.astype(jnp.float32)).astype(
                jnp.bfloat16
            )
        o_ref[r] = mixed


def depthwise(field, top, bottom, kernel, flip, add=None):
    rows, width, channels = field.shape
    lanes = LANES if channels % LANES == 0 else channels
    block = lambda n: pl.BlockSpec((n, width, lanes), lambda i: (0, 0, i))
    operands = [field, top, bottom, kernel]
    specs = [block(rows), block(3), block(3), pl.BlockSpec((7, 7, lanes), lambda i: (0, 0, i))]
    if add is not None:
        operands.append(add)
        specs.append(block(rows))
    return pl.pallas_call(
        functools.partial(conv_kernel, flip, add is not None),
        out_shape=jax.ShapeDtypeStruct(field.shape, jnp.bfloat16),
        grid=(channels // lanes,),
        in_specs=specs,
        out_specs=block(rows),
        scratch_shapes=[pltpu.VMEM((rows + 6, width + 16, lanes), jnp.float32)],
        compiler_params=pltpu.CompilerParams(vmem_limit_bytes=32 * 2**20),
        cost_estimate=pl.CostEstimate(
            flops=98 * rows * width * channels,
            bytes_accessed=6 * rows * width * channels,
            transcendentals=0,
        ),
        name="depthwise_flipped" if flip else "depthwise",
    )(*operands)


def halo(field):
    rows = field.shape[0]
    per_image = H // rows
    count = lax.axis_size("row")
    down = [(i, i + 1) for i in range(count - 1) if (i + 1) % per_image]
    up = [(j, i) for i, j in down]
    return lax.ppermute(field[-3:], "row", down), lax.ppermute(field[:3], "row", up)


def swap(value, distance):
    count = lax.axis_size("col")
    return lax.ppermute(value, "col", [(i, i ^ distance) for i in range(count)])


def gather_columns(piece):
    count = lax.axis_size("col")
    me = lax.axis_index("col")
    tokens, narrow = piece.shape
    out = jnp.zeros((tokens, narrow * count), piece.dtype)
    for distance in range(0, count, 2):
        arrived = swap(piece, distance) if distance else piece
        other = swap(arrived, 1)
        out = lax.dynamic_update_slice(out, arrived, (0, (me ^ distance) * narrow))
        out = lax.dynamic_update_slice(out, other, (0, (me ^ distance ^ 1) * narrow))
    return out


def scatter_columns(part):
    count = lax.axis_size("col")
    me = lax.axis_index("col")
    order = list(range(2, count, 2)) + [0]
    arrived = {d: swap(part(me ^ d ^ 1).astype(jnp.bfloat16), 1) for d in order}
    total = None
    pieces = []
    for d in order:
        pair = part(me ^ d) + arrived[d].astype(jnp.float32)
        pieces.append(swap(pair.astype(jnp.bfloat16), d).astype(jnp.float32) if d else pair)
    total = pieces[-1]
    for piece in pieces[:-1]:
        total = total + piece
    return total


def body(
    activations,
    cotangent,
    kernel,
    ln_gain,
    ln_bias,
    w_expand,
    b_expand,
    w_reduce,
    b_reduce,
    layer_scale,
):
    row_count, grid_width, narrow = activations.shape
    channels = narrow * lax.axis_size("col")
    col_start = lax.axis_index("col") * narrow
    tokens = row_count * grid_width
    units = w_expand.shape[1]
    step = units // CHUNKS
    dot = functools.partial(jnp.dot, preferred_element_type=jnp.float32)

    expand_full = lax.all_gather(w_expand, "row", axis=0, tiled=True)
    reduce_full = [
        lax.all_gather(w_reduce[i * step : (i + 1) * step], "row", axis=1, tiled=True)
        for i in range(CHUNKS)
    ]

    top, bottom = halo(activations)
    mixed_bf = depthwise(activations, top, bottom, kernel, False)
    local_mixed = mixed_bf.reshape(tokens, narrow).astype(jnp.float32)
    row_sum, square_sum = lax.psum(
        (jnp.sum(local_mixed, 1), jnp.sum(local_mixed * local_mixed, 1)), "col"
    )
    row_mean = row_sum[:, None] / channels
    square = square_sum[:, None] / channels
    inv_std = lax.rsqrt(square - row_mean * row_mean + epsilon)
    normal_local = (local_mixed - row_mean) * inv_std
    local_gain = lax.dynamic_slice_in_dim(ln_gain, col_start, narrow)
    local_shift = lax.dynamic_slice_in_dim(ln_bias, col_start, narrow)
    normed = (normal_local * local_gain + local_shift).astype(jnp.bfloat16)
    normed_full = gather_columns(normed)

    cot_f = cotangent.astype(jnp.float32)
    grad_branch = (layer_scale * cot_f).reshape(tokens, narrow).astype(jnp.bfloat16)
    grad_full = gather_columns(grad_branch)

    preact = dot(normed_full, expand_full) + b_expand
    cumulative = 0.5 * (1.0 + lax.erf(preact * root_half))
    hidden = (preact * cumulative).astype(jnp.bfloat16)
    slope = cumulative + preact * jnp.exp(-0.5 * preact * preact) * density_scale

    grad_parts = []
    for i in range(CHUNKS):
        grad_hidden = lax.dot_general(
            grad_full, reduce_full[i], (((1,), (1,)), ((), ())), preferred_element_type=jnp.float32
        )
        grad_parts.append(
            (grad_hidden * slope[:, i * step : (i + 1) * step]).astype(jnp.bfloat16)
        )
    grad_preact = jnp.concatenate(grad_parts, 1)

    def grad_part(owner):
        rows = lax.dynamic_slice_in_dim(expand_full, owner * narrow, narrow, 0)
        return lax.dot_general(
            grad_preact, rows, (((1,), (1,)), ((), ())), preferred_element_type=jnp.float32
        )

    def branch_part(owner):
        total = 0.0
        for i in range(CHUNKS):
            block = lax.dynamic_slice_in_dim(reduce_full[i], owner * narrow, narrow, 1)
            total = total + dot(hidden[:, i * step : (i + 1) * step], block)
        return total

    grad_gain = scatter_columns(grad_part) * local_gain
    branch_out = scatter_columns(branch_part) + b_reduce

    grad_sums = jnp.stack([jnp.sum(grad_gain, 1), jnp.sum(grad_gain * normal_local, 1)])
    every_sum = grad_sums
    for distance in range(1, lax.axis_size("col")):
        every_sum = every_sum + swap(grad_sums, distance)
    grad_total, grad_cross = every_sum[0], every_sum[1]
    grad_mixed = inv_std * (
        grad_gain - grad_total[:, None] / channels - normal_local * grad_cross[:, None] / channels
    )
    grad_mixed = grad_mixed.astype(jnp.bfloat16).reshape(row_count, grid_width, narrow)
    top, bottom = halo(grad_mixed)
    grad_input = depthwise(grad_mixed, top, bottom, kernel, True, cotangent)

    act_f = activations.astype(jnp.float32)
    block_out = (act_f + layer_scale * branch_out.reshape(row_count, grid_width, narrow)).astype(
        jnp.bfloat16
    )
    return (block_out, grad_input)


def solution(mesh):
    return jax.shard_map(
        body,
        mesh=mesh,
        in_specs=(
            P("row", None, "col"),
            P("row", None, "col"),
            P(None, None, "col"),
            P(),
            P(),
            P("row", "col"),
            P("col"),
            P("col", "row"),
            P("col"),
            P("col"),
        ),
        out_specs=(P("row", None, "col"), P("row", None, "col")),
        check_vma=False,
    )
```

```python
import functools

import jax
import jax.numpy as jnp
from jax import lax
from jax.experimental import pallas as pl
from jax.experimental.pallas import tpu as pltpu
from jax.sharding import PartitionSpec as P

H = 48
LANES = 128

epsilon = 1e-06
root_half = 0.7071067811865476
density_scale = 0.3989422804014327


def conv_kernel(flip, add, x_ref, top_ref, bottom_ref, k_ref, *rest):
    if add:
        add_ref, o_ref, field = rest
    else:
        o_ref, field = rest
    rows, width, lanes = x_ref.shape
    field[...] = jnp.zeros_like(field)
    field[0:3, 8 : 8 + width, :] = top_ref[...].astype(jnp.float32)
    field[3 : 3 + rows, 8 : 8 + width, :] = x_ref[...].astype(jnp.float32)
    field[3 + rows : 6 + rows, 8 : 8 + width, :] = bottom_ref[...].astype(jnp.float32)

    @pl.loop(0, rows)
    def _(r):
        total = jnp.zeros((width, lanes), jnp.float32)
        for a in range(7):
            for b in range(7):
                weight = k_ref[6 - a, 6 - b] if flip else k_ref[a, b]
                total += weight[None, :] * field[r + a, 5 + b : 5 + b + width, :]
        mixed = total.astype(jnp.bfloat16)
        if add:
            mixed = (add_ref[r].astype(jnp.float32) + mixed.astype(jnp.float32)).astype(
                jnp.bfloat16
            )
        o_ref[r] = mixed


def depthwise(field, top, bottom, kernel, flip, add=None):
    rows, width, channels = field.shape
    lanes = LANES if channels % LANES == 0 else channels
    block = lambda n: pl.BlockSpec((n, width, lanes), lambda i: (0, 0, i))
    operands = [field, top, bottom, kernel]
    specs = [block(rows), block(3), block(3), pl.BlockSpec((7, 7, lanes), lambda i: (0, 0, i))]
    if add is not None:
        operands.append(add)
        specs.append(block(rows))
    return pl.pallas_call(
        functools.partial(conv_kernel, flip, add is not None),
        out_shape=jax.ShapeDtypeStruct(field.shape, jnp.bfloat16),
        grid=(channels // lanes,),
        in_specs=specs,
        out_specs=block(rows),
        scratch_shapes=[pltpu.VMEM((rows + 6, width + 16, lanes), jnp.float32)],
        compiler_params=pltpu.CompilerParams(vmem_limit_bytes=32 * 2**20),
        cost_estimate=pl.CostEstimate(
            flops=98 * rows * width * channels,
            bytes_accessed=6 * rows * width * channels,
            transcendentals=0,
        ),
        name="depthwise_flipped" if flip else "depthwise",
    )(*operands)


def halo(field):
    rows = field.shape[0]
    per_image = H // rows
    count = lax.axis_size("row")
    down = [(i, i + 1) for i in range(count - 1) if (i + 1) % per_image]
    up = [(j, i) for i, j in down]
    return lax.ppermute(field[-3:], "row", down), lax.ppermute(field[:3], "row", up)


def swap(value, distance):
    count = lax.axis_size("col")
    return lax.ppermute(value, "col", [(i, i ^ distance) for i in range(count)])


def gather_columns(piece):
    count = lax.axis_size("col")
    me = lax.axis_index("col")
    tokens, narrow = piece.shape
    out = jnp.zeros((tokens, narrow * count), piece.dtype)
    for distance in range(0, count, 2):
        arrived = swap(piece, distance) if distance else piece
        other = swap(arrived, 1)
        out = lax.dynamic_update_slice(out, arrived, (0, (me ^ distance) * narrow))
        out = lax.dynamic_update_slice(out, other, (0, (me ^ distance ^ 1) * narrow))
    return out


def pair_sums(part):
    count = lax.axis_size("col")
    me = lax.axis_index("col")
    order = list(range(2, count, 2)) + [0]
    arrived = {d: swap(part(me ^ d ^ 1).astype(jnp.bfloat16), 1) for d in order}
    pairs = []
    for d in order:
        pair = part(me ^ d) + arrived[d].astype(jnp.float32)
        pairs.append(pair.astype(jnp.bfloat16) if d else pair)
    return pairs


def sum_pairs(pairs):
    total = pairs[-1]
    for index, pair in enumerate(pairs[:-1]):
        total = total + swap(pair, 2 * index + 2).astype(jnp.float32)
    return total


def body(
    activations,
    cotangent,
    kernel,
    ln_gain,
    ln_bias,
    w_expand,
    b_expand,
    w_reduce,
    b_reduce,
    layer_scale,
):
    row_count, grid_width, narrow = activations.shape
    channels = narrow * lax.axis_size("col")
    col_start = lax.axis_index("col") * narrow
    tokens = row_count * grid_width
    units = w_expand.shape[1]
    cut = narrow * 2 // 3
    dot = functools.partial(jnp.dot, preferred_element_type=jnp.float32)

    def turned(left, right):
        return lax.dot_general(
            left, right, (((1,), (1,)), ((), ())), preferred_element_type=jnp.float32
        )

    owners = w_reduce.reshape(units, -1, narrow)
    expand_full = lax.all_gather(w_expand, "row", axis=0, tiled=True)
    reduce_first = lax.all_gather(
        owners[:, :, :cut].reshape(units, -1), "row", axis=1, tiled=True
    )
    reduce_last = lax.all_gather(
        owners[:, :, cut:].reshape(units, -1), "row", axis=1, tiled=True
    )

    top, bottom = halo(activations)
    mixed_bf = depthwise(activations, top, bottom, kernel, False)
    local_mixed = mixed_bf.reshape(tokens, narrow).astype(jnp.float32)
    row_sum, square_sum = lax.psum(
        (jnp.sum(local_mixed, 1), jnp.sum(local_mixed * local_mixed, 1)), "col"
    )
    row_mean = row_sum[:, None] / channels
    square = square_sum[:, None] / channels
    inv_std = lax.rsqrt(square - row_mean * row_mean + epsilon)
    normal_local = (local_mixed - row_mean) * inv_std
    local_gain = lax.dynamic_slice_in_dim(ln_gain, col_start, narrow)
    local_shift = lax.dynamic_slice_in_dim(ln_bias, col_start, narrow)
    normed = (normal_local * local_gain + local_shift).astype(jnp.bfloat16)
    normed_full = gather_columns(normed)

    cot_f = cotangent.astype(jnp.float32)
    grad_branch = (layer_scale * cot_f).reshape(tokens, narrow).astype(jnp.bfloat16)
    grad_first = gather_columns(grad_branch[:, :cut])
    grad_last = gather_columns(grad_branch[:, cut:])
    expand_full, grad_first, grad_last = lax.optimization_barrier(
        (expand_full, grad_first, grad_last)
    )

    preact = dot(normed_full, expand_full) + b_expand
    cumulative = 0.5 * (1.0 + lax.erf(preact * root_half))
    hidden = (preact * cumulative).astype(jnp.bfloat16)

    def branch_part(weights, activated):
        width = weights.shape[1] // lax.axis_size("col")
        return lambda owner: dot(
            activated, lax.dynamic_slice_in_dim(weights, owner * width, width, 1)
        )

    branch_first = sum_pairs(pair_sums(branch_part(reduce_first, hidden)))
    grad_hidden = turned(grad_first, reduce_first)
    reduce_last, branch_first, grad_hidden = lax.optimization_barrier(
        (reduce_last, branch_first, grad_hidden)
    )
    slope = cumulative + preact * jnp.exp(-0.5 * preact * preact) * density_scale
    grad_hidden = grad_hidden + turned(grad_last, reduce_last)
    grad_preact = (grad_hidden * slope).astype(jnp.bfloat16)

    def grad_part(owner):
        return turned(
            grad_preact, lax.dynamic_slice_in_dim(expand_full, owner * narrow, narrow, 0)
        )

    grad_pairs = pair_sums(grad_part)
    *grad_pairs, hidden = lax.optimization_barrier((*grad_pairs, hidden))
    grad_gain = sum_pairs(grad_pairs) * local_gain
    branch_last = sum_pairs(pair_sums(branch_part(reduce_last, hidden)))
    branch_out = jnp.concatenate([branch_first, branch_last], 1) + b_reduce

    grad_sums = jnp.stack([jnp.sum(grad_gain, 1), jnp.sum(grad_gain * normal_local, 1)])
    every_sum = grad_sums
    for distance in range(1, lax.axis_size("col")):
        every_sum = every_sum + swap(grad_sums, distance)
    grad_total, grad_cross = every_sum[0], every_sum[1]
    grad_mixed = inv_std * (
        grad_gain - grad_total[:, None] / channels - normal_local * grad_cross[:, None] / channels
    )
    grad_mixed = grad_mixed.astype(jnp.bfloat16).reshape(row_count, grid_width, narrow)
    top, bottom = halo(grad_mixed)
    grad_input = depthwise(grad_mixed, top, bottom, kernel, True, cotangent)

    act_f = activations.astype(jnp.float32)
    block_out = (act_f + layer_scale * branch_out.reshape(row_count, grid_width, narrow)).astype(
        jnp.bfloat16
    )
    return (block_out, grad_input)


def solution(mesh):
    return jax.shard_map(
        body,
        mesh=mesh,
        in_specs=(
            P("row", None, "col"),
            P("row", None, "col"),
            P(None, None, "col"),
            P(),
            P(),
            P("row", "col"),
            P("col"),
            P("col", "row"),
            P("col"),
            P("col"),
        ),
        out_specs=(P("row", None, "col"), P("row", None, "col")),
        check_vma=False,
    )
```

```python
import functools

import jax
import jax.numpy as jnp
from jax import lax
from jax.experimental import pallas as pl
from jax.experimental.pallas import tpu as pltpu
from jax.sharding import PartitionSpec as P

H = 48
LANES = 128

epsilon = 1e-06
root_half = 0.7071067811865476
density_scale = 0.3989422804014327


def conv_kernel(flip, add, x_ref, top_ref, bottom_ref, k_ref, *rest):
    if add:
        add_ref, o_ref, field = rest
    else:
        o_ref, field = rest
    rows, width, lanes = x_ref.shape
    field[...] = jnp.zeros_like(field)
    field[0:3, 8 : 8 + width, :] = top_ref[...].astype(jnp.float32)
    field[3 : 3 + rows, 8 : 8 + width, :] = x_ref[...].astype(jnp.float32)
    field[3 + rows : 6 + rows, 8 : 8 + width, :] = bottom_ref[...].astype(jnp.float32)

    @pl.loop(0, rows)
    def _(r):
        total = jnp.zeros((width, lanes), jnp.float32)
        for a in range(7):
            for b in range(7):
                weight = k_ref[6 - a, 6 - b] if flip else k_ref[a, b]
                total += weight[None, :] * field[r + a, 5 + b : 5 + b + width, :]
        mixed = total.astype(jnp.bfloat16)
        if add:
            mixed = (add_ref[r].astype(jnp.float32) + mixed.astype(jnp.float32)).astype(
                jnp.bfloat16
            )
        o_ref[r] = mixed


def depthwise(field, top, bottom, kernel, flip, add=None):
    rows, width, channels = field.shape
    lanes = LANES if channels % LANES == 0 else channels
    block = lambda n: pl.BlockSpec((n, width, lanes), lambda i: (0, 0, i))
    operands = [field, top, bottom, kernel]
    specs = [block(rows), block(3), block(3), pl.BlockSpec((7, 7, lanes), lambda i: (0, 0, i))]
    if add is not None:
        operands.append(add)
        specs.append(block(rows))
    return pl.pallas_call(
        functools.partial(conv_kernel, flip, add is not None),
        out_shape=jax.ShapeDtypeStruct(field.shape, jnp.bfloat16),
        grid=(channels // lanes,),
        in_specs=specs,
        out_specs=block(rows),
        scratch_shapes=[pltpu.VMEM((rows + 6, width + 16, lanes), jnp.float32)],
        compiler_params=pltpu.CompilerParams(vmem_limit_bytes=32 * 2**20),
        cost_estimate=pl.CostEstimate(
            flops=98 * rows * width * channels,
            bytes_accessed=6 * rows * width * channels,
            transcendentals=0,
        ),
        name="depthwise_flipped" if flip else "depthwise",
    )(*operands)


def halo(field):
    rows = field.shape[0]
    per_image = H // rows
    count = lax.axis_size("row")
    down = [(i, i + 1) for i in range(count - 1) if (i + 1) % per_image]
    up = [(j, i) for i, j in down]
    return lax.ppermute(field[-3:], "row", down), lax.ppermute(field[:3], "row", up)


def swap(value, distance):
    count = lax.axis_size("col")
    return lax.ppermute(value, "col", [(i, i ^ distance) for i in range(count)])


def gather_rows(piece):
    count = lax.axis_size("row")
    me = lax.axis_index("row")
    depth, wide = piece.shape
    out = jnp.zeros((depth, wide * count), piece.dtype)
    for distance in range(count - 1, -1, -1):
        pairs = [(i, i ^ distance) for i in range(count)]
        arrived = lax.ppermute(piece, "row", pairs) if distance else piece
        out = lax.dynamic_update_slice(out, arrived, (0, (me ^ distance) * wide))
    return out


def gather_columns(piece):
    count = lax.axis_size("col")
    me = lax.axis_index("col")
    tokens, narrow = piece.shape
    out = jnp.zeros((tokens, narrow * count), piece.dtype)
    for distance in range(0, count, 2):
        arrived = swap(piece, distance) if distance else piece
        other = swap(arrived, 1)
        out = lax.dynamic_update_slice(out, arrived, (0, (me ^ distance) * narrow))
        out = lax.dynamic_update_slice(out, other, (0, (me ^ distance ^ 1) * narrow))
    return out


def pair_sums(part):
    count = lax.axis_size("col")
    me = lax.axis_index("col")
    order = list(range(count - 2, -1, -2))
    arrived = {d: swap(part(me ^ d ^ 1).astype(jnp.bfloat16), 1) for d in order}
    pairs = []
    for d in order:
        pair = part(me ^ d) + arrived[d].astype(jnp.float32)
        pairs.append(pair.astype(jnp.bfloat16) if d else pair)
    return pairs


def sum_pairs(pairs):
    total = pairs[-1]
    for index, pair in enumerate(reversed(pairs[:-1])):
        total = total + swap(pair, 2 * index + 2).astype(jnp.float32)
    return total


def body(
    activations,
    cotangent,
    kernel,
    ln_gain,
    ln_bias,
    w_expand,
    b_expand,
    w_reduce,
    b_reduce,
    layer_scale,
):
    row_count, grid_width, narrow = activations.shape
    channels = narrow * lax.axis_size("col")
    col_start = lax.axis_index("col") * narrow
    tokens = row_count * grid_width
    units = w_expand.shape[1]
    cut = narrow // 3
    dot = functools.partial(jnp.dot, preferred_element_type=jnp.float32)

    def turned(left, right):
        return lax.dot_general(
            left, right, (((1,), (1,)), ((), ())), preferred_element_type=jnp.float32
        )

    owners = w_reduce.reshape(units, -1, narrow)
    expand_full = lax.all_gather(w_expand, "row", axis=0, tiled=True)
    reduce_first = gather_rows(owners[:, :, :cut].reshape(units, -1))
    reduce_last = lax.all_gather(
        owners[:, :, cut:].reshape(units, -1), "row", axis=1, tiled=True
    )

    top, bottom = halo(activations)
    mixed_bf = depthwise(activations, top, bottom, kernel, False)
    local_mixed = mixed_bf.reshape(tokens, narrow).astype(jnp.float32)
    row_sum, square_sum = lax.psum(
        (jnp.sum(local_mixed, 1), jnp.sum(local_mixed * local_mixed, 1)), "col"
    )
    row_mean = row_sum[:, None] / channels
    square = square_sum[:, None] / channels
    inv_std = lax.rsqrt(square - row_mean * row_mean + epsilon)
    normal_local = (local_mixed - row_mean) * inv_std
    local_gain = lax.dynamic_slice_in_dim(ln_gain, col_start, narrow)
    local_shift = lax.dynamic_slice_in_dim(ln_bias, col_start, narrow)
    normed = (normal_local * local_gain + local_shift).astype(jnp.bfloat16)
    normed_full = gather_columns(normed)

    cot_f = cotangent.astype(jnp.float32)
    grad_branch = (layer_scale * cot_f).reshape(tokens, narrow).astype(jnp.bfloat16)
    grad_first = gather_columns(grad_branch[:, :cut])
    grad_last = gather_columns(grad_branch[:, cut:])
    expand_full, reduce_first, grad_first, grad_last = lax.optimization_barrier(
        (expand_full, reduce_first, grad_first, grad_last)
    )

    preact = dot(normed_full, expand_full) + b_expand
    cumulative = 0.5 * (1.0 + lax.erf(preact * root_half))
    hidden = (preact * cumulative).astype(jnp.bfloat16)

    def branch_part(weights, activated):
        width = weights.shape[1] // lax.axis_size("col")
        return lambda owner: dot(
            activated, lax.dynamic_slice_in_dim(weights, owner * width, width, 1)
        )

    branch_first = sum_pairs(pair_sums(branch_part(reduce_first, hidden)))
    grad_hidden = turned(grad_first, reduce_first)
    slope = cumulative + preact * jnp.exp(-0.5 * preact * preact) * density_scale
    vectors = jnp.stack([ln_gain, ln_bias])
    gain_unit, bias_unit = jnp.dot(
        vectors, expand_full.astype(jnp.float32), precision=lax.Precision.HIGHEST
    )
    scaled = preact - (b_expand + bias_unit)
    reduce_last, branch_first, grad_hidden, slope, gain_unit, scaled = lax.optimization_barrier(
        (reduce_last, branch_first, grad_hidden, slope, gain_unit, scaled)
    )
    grad_hidden = grad_hidden + turned(grad_last, reduce_last)
    grad_preact = (grad_hidden * slope).astype(jnp.bfloat16)

    def grad_part(owner):
        return turned(
            grad_preact, lax.dynamic_slice_in_dim(expand_full, owner * narrow, narrow, 0)
        )

    grad_pairs = pair_sums(grad_part)
    grad_float = grad_preact.astype(jnp.float32)
    grad_sums = jnp.stack(
        [jnp.sum(grad_float * gain_unit, 1), jnp.sum(grad_float * scaled, 1)]
    )
    distance = 1
    while distance < lax.axis_size("col"):
        grad_sums = grad_sums + swap(grad_sums, distance)
        distance *= 2
    grad_total, grad_cross = grad_sums[0], grad_sums[1]
    hidden = lax.optimization_barrier((hidden, *grad_pairs))[0]
    grad_gain = sum_pairs(grad_pairs) * local_gain
    branch_last = sum_pairs(pair_sums(branch_part(reduce_last, hidden)))
    branch_out = jnp.concatenate([branch_first, branch_last], 1) + b_reduce

    grad_mixed = inv_std * (
        grad_gain - grad_total[:, None] / channels - normal_local * grad_cross[:, None] / channels
    )
    grad_mixed = grad_mixed.astype(jnp.bfloat16).reshape(row_count, grid_width, narrow)
    top, bottom = halo(grad_mixed)
    grad_input = depthwise(grad_mixed, top, bottom, kernel, True, cotangent)

    act_f = activations.astype(jnp.float32)
    block_out = (act_f + layer_scale * branch_out.reshape(row_count, grid_width, narrow)).astype(
        jnp.bfloat16
    )
    return (block_out, grad_input)


def solution(mesh):
    return jax.shard_map(
        body,
        mesh=mesh,
        in_specs=(
            P("row", None, "col"),
            P("row", None, "col"),
            P(None, None, "col"),
            P(),
            P(),
            P("row", "col"),
            P("col"),
            P("col", "row"),
            P("col"),
            P("col"),
        ),
        out_specs=(P("row", None, "col"), P("row", None, "col")),
        check_vma=False,
    )
```

```python
import functools

import jax
import jax.numpy as jnp
from jax import lax
from jax.experimental import pallas as pl
from jax.experimental.pallas import tpu as pltpu
from jax.sharding import PartitionSpec as P

H = 48
LANES = 128

epsilon = 1e-06
root_half = 0.7071067811865476
density_scale = 0.3989422804014327


def conv_kernel(flip, add, x_ref, top_ref, bottom_ref, k_ref, *rest):
    if add:
        add_ref, o_ref, field = rest
    else:
        o_ref, field = rest
    rows, width, lanes = x_ref.shape
    field[...] = jnp.zeros_like(field)
    field[0:3, 8 : 8 + width, :] = top_ref[...].astype(jnp.float32)
    field[3 : 3 + rows, 8 : 8 + width, :] = x_ref[...].astype(jnp.float32)
    field[3 + rows : 6 + rows, 8 : 8 + width, :] = bottom_ref[...].astype(jnp.float32)

    @pl.loop(0, rows)
    def _(r):
        total = jnp.zeros((width, lanes), jnp.float32)
        for a in range(7):
            for b in range(7):
                weight = k_ref[6 - a, 6 - b] if flip else k_ref[a, b]
                total += weight[None, :] * field[r + a, 5 + b : 5 + b + width, :]
        mixed = total.astype(jnp.bfloat16)
        if add:
            mixed = (add_ref[r].astype(jnp.float32) + mixed.astype(jnp.float32)).astype(
                jnp.bfloat16
            )
        o_ref[r] = mixed


def depthwise(field, top, bottom, kernel, flip, add=None):
    rows, width, channels = field.shape
    lanes = LANES if channels % LANES == 0 else channels
    block = lambda n: pl.BlockSpec((n, width, lanes), lambda i: (0, 0, i))
    operands = [field, top, bottom, kernel]
    specs = [block(rows), block(3), block(3), pl.BlockSpec((7, 7, lanes), lambda i: (0, 0, i))]
    if add is not None:
        operands.append(add)
        specs.append(block(rows))
    return pl.pallas_call(
        functools.partial(conv_kernel, flip, add is not None),
        out_shape=jax.ShapeDtypeStruct(field.shape, jnp.bfloat16),
        grid=(channels // lanes,),
        in_specs=specs,
        out_specs=block(rows),
        scratch_shapes=[pltpu.VMEM((rows + 6, width + 16, lanes), jnp.float32)],
        compiler_params=pltpu.CompilerParams(vmem_limit_bytes=32 * 2**20),
        cost_estimate=pl.CostEstimate(
            flops=98 * rows * width * channels,
            bytes_accessed=6 * rows * width * channels,
            transcendentals=0,
        ),
        name="depthwise_flipped" if flip else "depthwise",
    )(*operands)


def halo(field):
    rows = field.shape[0]
    per_image = H // rows
    count = lax.axis_size("row")
    down = [(i, i + 1) for i in range(count - 1) if (i + 1) % per_image]
    up = [(j, i) for i, j in down]
    return lax.ppermute(field[-3:], "row", down), lax.ppermute(field[:3], "row", up)


def swap(value, distance):
    count = lax.axis_size("col")
    return lax.ppermute(value, "col", [(i, i ^ distance) for i in range(count)])


def gather_columns(piece):
    count = lax.axis_size("col")
    me = lax.axis_index("col")
    tokens, narrow = piece.shape
    out = jnp.zeros((tokens, narrow * count), piece.dtype)
    for distance in range(0, count, 2):
        arrived = swap(piece, distance) if distance else piece
        other = swap(arrived, 1)
        out = lax.dynamic_update_slice(out, arrived, (0, (me ^ distance) * narrow))
        out = lax.dynamic_update_slice(out, other, (0, (me ^ distance ^ 1) * narrow))
    return out


def pair_sums(part, operand):
    count = lax.axis_size("col")
    me = lax.axis_index("col")
    order = list(range(count - 2, -1, -2))
    arrived = {}
    pairs = []

    def send(d):
        nonlocal operand
        term = part(operand, me ^ d ^ 1).astype(jnp.bfloat16)
        operand, term = lax.optimization_barrier((operand, term))
        arrived[d] = swap(term, 1)

    def add(d):
        nonlocal operand
        pair = part(operand, me ^ d) + arrived[d].astype(jnp.float32)
        pair = pair.astype(jnp.bfloat16) if d else pair
        operand, pair = lax.optimization_barrier((operand, pair))
        pairs.append(pair)

    ahead = min(3, len(order))
    for d in order[:ahead]:
        send(d)
    for index, d in enumerate(order):
        add(d)
        if index >= 1 and index + ahead - 1 < len(order):
            send(order[index + ahead - 1])
    return pairs, operand


def exchange(pairs):
    count = lax.axis_size("col")
    return [swap(pair, count - 2 - 2 * i) for i, pair in enumerate(pairs[:-1])]


def sum_pairs(pairs, received=None):
    received = exchange(pairs) if received is None else received
    total = pairs[-1]
    for piece in received:
        total = total + piece.astype(jnp.float32)
    return total


def body(
    activations,
    cotangent,
    kernel,
    ln_gain,
    ln_bias,
    w_expand,
    b_expand,
    w_reduce,
    b_reduce,
    layer_scale,
):
    row_count, grid_width, narrow = activations.shape
    channels = narrow * lax.axis_size("col")
    col_start = lax.axis_index("col") * narrow
    tokens = row_count * grid_width
    units = w_expand.shape[1]
    cut = narrow * 2 // 3
    dot = functools.partial(jnp.dot, preferred_element_type=jnp.float32)

    def turned(left, right):
        return lax.dot_general(
            left, right, (((1,), (1,)), ((), ())), preferred_element_type=jnp.float32
        )

    owners = w_reduce.reshape(units, -1, narrow)
    expand_full = lax.all_gather(w_expand, "row", axis=0, tiled=True)
    reduce_first = lax.all_gather(
        owners[:, :, :cut].reshape(units, -1), "row", axis=1, tiled=True
    )
    reduce_last = lax.all_gather(
        owners[:, :, cut:].reshape(units, -1), "row", axis=1, tiled=True
    )

    top, bottom = halo(activations)
    mixed_bf = depthwise(activations, top, bottom, kernel, False)
    local_mixed = mixed_bf.reshape(tokens, narrow).astype(jnp.float32)
    row_sum, square_sum = lax.psum(
        (jnp.sum(local_mixed, 1), jnp.sum(local_mixed * local_mixed, 1)), "col"
    )
    row_mean = row_sum[:, None] / channels
    square = square_sum[:, None] / channels
    inv_std = lax.rsqrt(square - row_mean * row_mean + epsilon)
    normal_local = (local_mixed - row_mean) * inv_std
    local_gain = lax.dynamic_slice_in_dim(ln_gain, col_start, narrow)
    local_shift = lax.dynamic_slice_in_dim(ln_bias, col_start, narrow)
    normed = (normal_local * local_gain + local_shift).astype(jnp.bfloat16)
    normed_full = gather_columns(normed)

    cot_f = cotangent.astype(jnp.float32)
    grad_branch = (layer_scale * cot_f).reshape(tokens, narrow).astype(jnp.bfloat16)
    grad_first = gather_columns(grad_branch[:, :cut])
    grad_last = gather_columns(grad_branch[:, cut:])
    expand_full, grad_first, grad_last = lax.optimization_barrier(
        (expand_full, grad_first, grad_last)
    )

    preact = dot(normed_full, expand_full) + b_expand
    cumulative = 0.5 * (1.0 + lax.erf(preact * root_half))
    hidden = (preact * cumulative).astype(jnp.bfloat16)

    def branch_part(weights, activated):
        width = weights.shape[1] // lax.axis_size("col")
        return pair_sums(
            lambda operand, owner: dot(
                operand, lax.dynamic_slice_in_dim(weights, owner * width, width, 1)
            ),
            activated,
        )[0]

    branch_first = sum_pairs(branch_part(reduce_first, hidden))
    grad_hidden = turned(grad_first, reduce_first)
    slope = cumulative + preact * jnp.exp(-0.5 * preact * preact) * density_scale
    vectors = jnp.stack([ln_gain, ln_bias])
    gain_unit, bias_unit = jnp.dot(
        vectors, expand_full.astype(jnp.float32), precision=lax.Precision.HIGHEST
    )
    scaled = preact - (b_expand + bias_unit)
    reduce_last, branch_first, grad_hidden, slope, gain_unit, scaled = lax.optimization_barrier(
        (reduce_last, branch_first, grad_hidden, slope, gain_unit, scaled)
    )
    grad_hidden = grad_hidden + turned(grad_last, reduce_last)
    grad_preact = (grad_hidden * slope).astype(jnp.bfloat16)

    def grad_part(operand, owner):
        return turned(operand, lax.dynamic_slice_in_dim(expand_full, owner * narrow, narrow, 0))

    grad_pairs, grad_preact = pair_sums(grad_part, grad_preact)
    grad_float = grad_preact.astype(jnp.float32)
    grad_sums = jnp.stack(
        [jnp.sum(grad_float * gain_unit, 1), jnp.sum(grad_float * scaled, 1)]
    )
    distance = 1
    while distance < lax.axis_size("col"):
        grad_sums = grad_sums + swap(grad_sums, distance)
        distance *= 2
    grad_total, grad_cross = grad_sums[0], grad_sums[1]
    received = exchange(grad_pairs)
    hidden = lax.optimization_barrier((hidden, *received[:-1], grad_pairs[-1]))[0]
    grad_gain = sum_pairs(grad_pairs, received) * local_gain
    branch_last = sum_pairs(branch_part(reduce_last, hidden))
    branch_out = jnp.concatenate([branch_first, branch_last], 1) + b_reduce

    grad_mixed = inv_std * (
        grad_gain - grad_total[:, None] / channels - normal_local * grad_cross[:, None] / channels
    )
    grad_mixed = grad_mixed.astype(jnp.bfloat16).reshape(row_count, grid_width, narrow)
    top, bottom = halo(grad_mixed)
    grad_input = depthwise(grad_mixed, top, bottom, kernel, True, cotangent)

    act_f = activations.astype(jnp.float32)
    block_out = (act_f + layer_scale * branch_out.reshape(row_count, grid_width, narrow)).astype(
        jnp.bfloat16
    )
    return (block_out, grad_input)


def solution(mesh):
    return jax.shard_map(
        body,
        mesh=mesh,
        in_specs=(
            P("row", None, "col"),
            P("row", None, "col"),
            P(None, None, "col"),
            P(),
            P(),
            P("row", "col"),
            P("col"),
            P("col", "row"),
            P("col"),
            P("col"),
        ),
        out_specs=(P("row", None, "col"), P("row", None, "col")),
        check_vma=False,
    )
```
